128 devices in a mesh: wide: 32 (over y, z, core), narrow: 4 (over x).
Axes of the slice: x: 4, y: 4, z: 4, core: 2. Of those that a mesh axis runs over, the one named last changes fastest.
Arguments:
- frames: bfloat16 [256, 2, 256, 256], P(('wide', 'narrow')), may hold values from -120 to 120
- sketch: bfloat16 [256, 128], replicated, may hold values from -0.3 to 2.3
- kernel_taps: bfloat16 [64], replicated, may hold values from -0.3 to 1.1
Outputs:
- basis: float32 [128, 32768], P(None, ('wide', 'narrow'))
- factor: float32 [128, 128], replicated
The draws below stay inside these ranges and needn't reach their ends.
All inputs are finite; a program needn't handle non-finite values.
Results may differ from the reference program's by a relative error of at most 0.0043.
Values may be sent and summed in bfloat16 or wider, within the bound.
A program may use at most 64 MiB of HBM per device.

```python
import math
import jax
import jax.numpy as jnp
from jax import lax

PLANES = 2
ROWS = 256
COLS = 256
TIME = 256
RANK = 128
NTAP = 64
VOXELS = 32768


def draw_frames(key, part):
    key_noise, key_rows, key_times = jax.random.split(key, 3)
    layout = (TIME, PLANES, ROWS, COLS)
    noise = jax.random.truncated_normal(key_noise, -4.0, 4.0, layout, jnp.float32)
    row_scale = jnp.exp(jax.random.uniform(key_rows, (1, PLANES, ROWS, 1), jnp.float32, 0.0, math.log(10.0)))
    time_scale = jnp.exp(jax.random.uniform(key_times, (TIME, 1, 1, 1), jnp.float32, 0.0, math.log(2.0)))
    values = noise * row_scale * time_scale
    return values.astype(jnp.bfloat16)


def draw_sketch(key, part):
    spread = 1.0 / (math.sqrt(TIME) + math.sqrt(RANK))
    random_part = jax.random.truncated_normal(key, -4.0, 4.0, (TIME, RANK), jnp.float32) * spread
    diagonal = jnp.arange(TIME, dtype=jnp.int32)[:, None] == jnp.arange(RANK, dtype=jnp.int32)[None, :]
    return (random_part + jnp.where(diagonal, jnp.float32(2.0), jnp.float32(0.0))).astype(jnp.bfloat16)


def draw_kernel_taps(key, part):
    key_lead, key_rest = jax.random.split(key, 2)
    position = jnp.arange(NTAP, dtype=jnp.float32)
    weights = jnp.exp(-(position - 1.0) / 16.0) / 16.5
    rest = jax.random.uniform(key_rest, (NTAP,), jnp.float32, -1.0, 1.0) * 0.3 * weights
    lead = jax.random.uniform(key_lead, (NTAP,), jnp.float32, 0.9, 1.1)
    return jnp.where(position < 0.5, lead, rest).astype(jnp.bfloat16)


def setup_inputs(seed: int = 0) -> dict:
    streams_of = jax.random.split(jax.random.key(seed), 4)
    return {
        "frames": draw_frames(jax.random.fold_in(streams_of[3], 71), 0),
        "sketch": draw_sketch(jax.random.fold_in(streams_of[3], 71), 0),
        "kernel_taps": draw_kernel_taps(jax.random.fold_in(streams_of[3], 71), 0),
    }


def gauss_taps(spread):
    position = jnp.arange(15, dtype=jnp.float32) - 7.0
    weights = jnp.exp(-position * position / (2.0 * spread * spread))
    return weights / jnp.sum(weights)

def band_matrix(spread, length):
    outputs = length // 2
    offset_index = jnp.arange(length, dtype=jnp.int32)[None, :] - 2 * jnp.arange(outputs, dtype=jnp.int32)[:, None] + 7
    weights = gauss_taps(spread)
    matrix = jnp.zeros((outputs, length), jnp.float32)
    for offset in range(15):
        matrix = matrix + jnp.where(offset_index == offset, weights[offset], jnp.float32(0.0))
    return matrix

def filter_volumes(frames_block):
    volume = frames_block.astype(jnp.float32)
    row_count = volume.shape[-2]
    col_count = volume.shape[-1]
    half = col_count // 2
    column_bands = jnp.concatenate([band_matrix(1.5, col_count), band_matrix(3.0, col_count)], axis=0)
    column_pass = jnp.einsum('...rc,oc->...ro', volume, column_bands, precision=lax.Precision.HIGHEST)
    narrow_pass = jnp.einsum('or,...rc->...oc', band_matrix(1.5, row_count), column_pass[..., :half], precision=lax.Precision.HIGHEST)
    broad_pass = jnp.einsum('or,...rc->...oc', band_matrix(3.0, row_count), column_pass[..., half:], precision=lax.Precision.HIGHEST)
    return (narrow_pass - broad_pass).astype(jnp.bfloat16)

def build_toeplitz(kernel_taps, length):
    lag_index = jnp.arange(length, dtype=jnp.int32)[:, None] - jnp.arange(length, dtype=jnp.int32)[None, :]
    toeplitz = jnp.zeros((length, length), jnp.float32)
    for offset in range(kernel_taps.shape[0]):
        toeplitz = toeplitz + jnp.where(lag_index == offset, kernel_taps[offset].astype(jnp.float32), jnp.float32(0.0))
    return toeplitz.astype(jnp.bfloat16)

def orthonormalize(sketched, voxel_count):
    gram_part = lax.dot_general(sketched.astype(jnp.float32), sketched.astype(jnp.float32), (((1,), (1,)), ((), ())), precision=lax.Precision.HIGHEST, preferred_element_type=jnp.float32) / voxel_count
    lower_factor = jnp.linalg.cholesky(gram_part)
    basis_rows = jax.scipy.linalg.solve_triangular(lower_factor, sketched, lower=True)
    return (basis_rows, lower_factor.T)

def reference(frames, sketch, kernel_taps):
    filtered = lax.map(filter_volumes, frames).reshape(TIME, VOXELS)
    toeplitz = build_toeplitz(kernel_taps, TIME)
    deconvolved = jnp.dot(toeplitz.astype(jnp.float32), filtered.astype(jnp.float32), preferred_element_type=jnp.float32).astype(jnp.bfloat16)
    sketched = lax.dot_general(sketch.astype(jnp.float32), deconvolved.astype(jnp.float32), (((0,), (0,)), ((), ())), preferred_element_type=jnp.float32)
    first_basis, unused = orthonormalize(sketched, VOXELS)
    series = deconvolved.astype(jnp.float32)
    projected = lax.dot_general(series.astype(jnp.float32), first_basis.astype(jnp.float32), (((1,), (1,)), ((), ())), precision=lax.Precision.HIGHEST, preferred_element_type=jnp.float32) / VOXELS
    refined = lax.dot_general(projected.astype(jnp.float32), series.astype(jnp.float32), (((0,), (0,)), ((), ())), precision=lax.Precision.HIGHEST, preferred_element_type=jnp.float32)
    basis, factor = orthonormalize(refined, VOXELS)
    return (basis, factor)
```

```python
import functools

import jax
import jax.numpy as jnp
import numpy as np
from jax import lax
from jax.experimental import pallas as pl
from jax.experimental.pallas import tpu as pltpu
from jax.sharding import PartitionSpec as P

MESH = pl.DeviceIdType.MESH
F32 = jnp.float32
BF16 = jnp.bfloat16


def gauss_band(spread, length):
    position = np.arange(15, dtype=np.float64) - 7.0
    weights = np.exp(-position * position / (2.0 * spread * spread))
    weights = weights / weights.sum()
    matrix = np.zeros((length // 2, length), np.float64)
    for o in range(length // 2):
        for k in range(15):
            c = 2 * o + k - 7
            if 0 <= c < length:
                matrix[o, c] = weights[k]
    return matrix


def split2(matrix):
    hi = matrix.astype(BF16)
    lo = (matrix - hi.astype(F32)).astype(BF16)
    return hi, lo


def split3(matrix):
    hi = matrix.astype(BF16)
    rest = matrix - hi.astype(F32)
    mid = rest.astype(BF16)
    lo = (rest - mid.astype(F32)).astype(BF16)
    return hi, mid, lo


def np_split2(matrix):
    hi = matrix.astype(BF16)
    lo = (matrix - hi.astype(np.float64)).astype(BF16)
    return hi, lo


def dot(a, b, ca=1, cb=0):
    return lax.dot_general(a, b, (((ca,), (cb,)), ((), ())), preferred_element_type=F32)


def dot_ff(a, b, ca=1, cb=0):
    ah, al = split2(a)
    bh, bl = split2(b)
    return dot(ah, bh, ca, cb) + (dot(ah, bl, ca, cb) + dot(al, bh, ca, cb))


def dot_fb(a, b, ca=1, cb=0):
    hi, mid, lo = split3(a)
    return dot(hi, b, ca, cb) + (dot(mid, b, ca, cb) + dot(lo, b, ca, cb))


def exchange_kernel(
    n_wide, n_narrow, frames_ref, taps_ref, colh_ref, coll_ref, rowh_ref, rowl_ref,
    gram_ref, series_ref,
    tap_row, tx, rx, gtx, grx, gall, send_sems, recv_sems,
):
    n = n_wide * n_narrow
    me = lax.axis_index("wide") * n_narrow + lax.axis_index("narrow")

    def peer(i):
        p = lax.rem(me + i, n)
        return p, (p // n_narrow, lax.rem(p, n_narrow))

    barrier = pltpu.get_barrier_semaphore()

    def greet(i, carry):
        _, device = peer(i)
        pl.semaphore_signal(barrier, inc=1, device_id=device, device_id_type=MESH)
        return carry

    lax.fori_loop(1, n, greet, 0)

    x = frames_ref[...].reshape(2 * 2 * 256, 256)
    y = dot(x, colh_ref[...]) + dot(x, coll_ref[...])
    for p in range(2):
        a = y[p * 256 : (p + 1) * 256]
        b = y[(p + 2) * 256 : (p + 3) * 256]
        right = jnp.concatenate(
            [
                jnp.concatenate([a[:, :128], b[:, :128]], axis=1),
                jnp.concatenate([a[:, 128:], b[:, 128:]], axis=1),
            ],
            axis=0,
        )
        rh, rl = split2(right)
        out = dot(rowh_ref[...], rh) + (dot(rowh_ref[...], rl) + dot(rowl_ref[...], rh))
        out = out.astype(BF16).astype(F32)
        for h in range(2):
            tx[p * 64 : (p + 1) * 64, 0, h * 256 : (h + 1) * 256] = out[h * 64 : (h + 1) * 64]

    pl.semaphore_wait(barrier, n - 1)

    def push(src, dst, slot):
        def body(i, carry):
            p, device = peer(i)
            pltpu.make_async_remote_copy(
                src_ref=src.at[p],
                dst_ref=dst.at[me],
                send_sem=send_sems.at[slot],
                recv_sem=recv_sems.at[slot],
                device_id=device,
                device_id_type=MESH,
            ).start()
            return carry

        lax.fori_loop(1, n, body, 0)

    def wait(ref, sem):
        part = ref.at[pl.ds(0, n - 1)]
        pltpu.make_async_copy(part, part, sem).wait()

    push(tx, rx, 0)
    rx[me] = tx[me]

    tap_row[...] = jnp.zeros_like(tap_row)
    tap_row[0:1, 0:64] = taps_ref[...].astype(F32)
    base = jnp.broadcast_to(tap_row[0:1, :], (128, 256))
    s_index = lax.broadcasted_iota(jnp.int32, (128, 256), 0)
    t_index = lax.broadcasted_iota(jnp.int32, (128, 256), 1)
    halves = []
    for v in range(2):
        rolled = pltpu.roll(base, v, 1, stride=2, stride_axis=0)
        halves.append(jnp.where(t_index >= 2 * s_index + v, rolled, 0.0))
    toeplitz = jnp.concatenate(halves, axis=0).astype(BF16)

    wait(rx, recv_sems.at[0])
    columns = [
        jnp.concatenate([rx[:, 0, (2 * h + v) * 128 : (2 * h + v + 1) * 128] for v in range(2)], axis=0)
        for h in range(2)
    ]
    received = jnp.concatenate(columns, axis=1).astype(BF16)
    series = dot(toeplitz, received, 0, 0).astype(BF16)
    series_ref[...] = series
    part = dot(series, series, 1, 1)
    gtx[:, 0, 0:128] = part[0:128, 0:128]
    gtx[:, 0, 128:256] = part[128:256, 0:128]
    gtx[:, 0, 256:384] = part[128:256, 128:256]
    push(gtx, grx, 1)
    grx[me] = gtx[me]
    wait(grx, recv_sems.at[1])
    gall[me] = jnp.sum(grx[...], axis=0)

    def share(i, carry):
        _, device = peer(i)
        pltpu.make_async_remote_copy(
            src_ref=gall.at[me],
            dst_ref=gall.at[me],
            send_sem=send_sems.at[2],
            recv_sem=recv_sems.at[2],
            device_id=device,
            device_id_type=MESH,
        ).start()
        return carry

    lax.fori_loop(1, n, share, 0)
    wait(gall, recv_sems.at[2])
    gram_ref[...] = gall[:, 0, :] * (1.0 / 32768.0)
    wait(tx, send_sems.at[0])
    wait(gtx, send_sems.at[1])
    wait(gall, send_sems.at[2])


def eliminate(matrices):
    size = matrices[0].shape[0]
    r = lax.broadcasted_iota(jnp.int32, (size, size), 0)
    c = lax.broadcasted_iota(jnp.int32, (size, size), 1)
    eye = jnp.where(r == c, 1.0, 0.0).astype(F32)
    sub = lax.broadcasted_iota(jnp.int32, (8, 1), 0)
    work = []
    for g in matrices:
        m = jnp.concatenate([g, eye], axis=1)
        work.append([m[8 * i : 8 * i + 8] for i in range(size // 8)])
    for k in range(size):
        t, s = divmod(k, 8)
        for rows in work:
            row = rows[t][s : s + 1, :]
            scaled = row * (1.0 / row[:, k : k + 1])
            for i in range(t, size // 8):
                f = rows[i][:, k : k + 1]
                if i == t:
                    f = jnp.where(sub > s, f, 0.0)
                rows[i] = rows[i] - f * scaled
    results = []
    for rows in work:
        m = jnp.concatenate(rows, axis=0)
        upper = jnp.where(c >= r, m[:, :size], 0.0)
        diagonal = jnp.sum(jnp.where(r == c, upper, 0.0), axis=1, keepdims=True)
        scale = lax.rsqrt(diagonal)
        results.append((upper * scale, m[:, size:] * scale))
    return results


def factor_kernel(gram_ref, series_ref, sketch_ref, basis_ref, factor_ref):
    c11 = gram_ref[:, 0:128]
    c21 = gram_ref[:, 128:256]
    c22 = gram_ref[:, 256:384]
    cov = jnp.concatenate(
        [jnp.concatenate([c11, c21.T], axis=1), jnp.concatenate([c21, c22], axis=1)], axis=0
    )
    sketch = sketch_ref[...]
    w = dot_fb(cov, sketch)
    g1 = dot_fb(w, sketch, 0, 0).T
    cw = dot_ff(cov, w)
    g2 = dot_ff(w, cw, 0, 0)
    (_, inv1), (up2, inv2) = eliminate([g1, g2])
    factor_ref[...] = dot_ff(up2, inv1, 1, 1)
    z = dot_ff(inv2, w, 1, 1)
    basis_ref[...] = dot_fb(z, series_ref[...])


def shards(n_wide, n_narrow, frames, sketch, kernel_taps):
    n = n_wide * n_narrow
    narrow_band, broad_band = gauss_band(1.5, 256), gauss_band(3.0, 256)
    colh, coll = np_split2(np.concatenate([narrow_band, broad_band], axis=0).T)
    order = np.concatenate([np.arange(0, 128, 2), np.arange(1, 128, 2)])
    rowh, rowl = np_split2(np.concatenate([narrow_band, -broad_band], axis=1)[order])
    vmem = pl.BlockSpec(memory_space=pltpu.VMEM)
    gram, series = pl.pallas_call(
        functools.partial(exchange_kernel, n_wide, n_narrow),
        out_shape=(
            jax.ShapeDtypeStruct((128, 384), F32),
            jax.ShapeDtypeStruct((256, 256), BF16),
        ),
        in_specs=[vmem] * 6,
        out_specs=(vmem, vmem),
        scratch_shapes=[
            pltpu.VMEM((8, 256), F32),
            pltpu.VMEM((n, 1, 512), F32),
            pltpu.VMEM((n, 1, 512), F32),
            pltpu.VMEM((n, 1, 384), F32),
            pltpu.VMEM((n, 1, 384), F32),
            pltpu.VMEM((n, 1, 384), F32),
            pltpu.SemaphoreType.DMA((3,)),
            pltpu.SemaphoreType.DMA((3,)),
        ],
        compiler_params=pltpu.CompilerParams(
            collective_id=0, has_side_effects=True, vmem_limit_bytes=40 * 2**20
        ),
        name="exchange",
    )(
        frames, kernel_taps.reshape(1, 64),
        jnp.asarray(colh), jnp.asarray(coll), jnp.asarray(rowh), jnp.asarray(rowl),
    )
    return pl.pallas_call(
        factor_kernel,
        out_shape=(jax.ShapeDtypeStruct((128, 256), F32), jax.ShapeDtypeStruct((128, 128), F32)),
        in_specs=[vmem] * 3,
        out_specs=(vmem, vmem),
        compiler_params=pltpu.CompilerParams(vmem_limit_bytes=40 * 2**20),
        name="factorize",
    )(gram, series, sketch)


def solution(mesh):
    return jax.shard_map(
        functools.partial(shards, mesh.shape["wide"], mesh.shape["narrow"]),
        mesh=mesh,
        in_specs=(P(("wide", "narrow"), None, None, None), P(), P()),
        out_specs=(P(None, ("wide", "narrow")), P()),
        check_vma=False,
    )
```

```python
import jax
import jax.numpy as jnp
import numpy as np
from jax import lax
from jax.experimental import pallas as pl
from jax.experimental.pallas import tpu as pltpu
from jax.sharding import PartitionSpec as P

MESH = pl.DeviceIdType.MESH
F32 = jnp.float32
BF16 = jnp.bfloat16


def gauss_band(spread, length):
    position = np.arange(15, dtype=np.float64) - 7.0
    weights = np.exp(-position * position / (2.0 * spread * spread))
    weights = weights / weights.sum()
    matrix = np.zeros((length // 2, length), np.float64)
    for o in range(length // 2):
        for k in range(15):
            c = 2 * o + k - 7
            if 0 <= c < length:
                matrix[o, c] = weights[k]
    return matrix


def split2(matrix):
    hi = matrix.astype(BF16)
    lo = (matrix - hi.astype(F32)).astype(BF16)
    return hi, lo


def split3(matrix):
    hi = matrix.astype(BF16)
    rest = matrix - hi.astype(F32)
    mid = rest.astype(BF16)
    lo = (rest - mid.astype(F32)).astype(BF16)
    return hi, mid, lo


def np_split2(matrix):
    hi = matrix.astype(BF16)
    lo = (matrix - hi.astype(np.float64)).astype(BF16)
    return hi, lo


def dot(a, b, ca=1, cb=0):
    return lax.dot_general(a, b, (((ca,), (cb,)), ((), ())), preferred_element_type=F32)


def dot_ff(a, b, ca=1, cb=0):
    ah, am, al = split3(a)
    bh, bm, bl = split3(b)
    first = dot(ah, bm, ca, cb) + dot(am, bh, ca, cb)
    second = dot(ah, bl, ca, cb) + dot(am, bm, ca, cb) + dot(al, bh, ca, cb)
    return dot(ah, bh, ca, cb) + (first + second)


def dot_fb(a, b, ca=1, cb=0):
    hi, mid, lo = split3(a)
    return dot(hi, b, ca, cb) + (dot(mid, b, ca, cb) + dot(lo, b, ca, cb))


def hops(*offsets):
    return sum(min(o % 4, -o % 4) for o in offsets)


YZ = sorted(((y, z) for y in range(4) for z in range(4) if y or z), key=lambda s: -hops(*s))
CX = sorted(((c, x) for c in range(2) for x in range(4) if c or x), key=lambda s: (-hops(s[1]), -s[0]))


def exchange_kernel(
    frames_hbm, taps_hbm, bands_hbm,
    gram_ref, series_ref,
    frames_ref, taps_ref, bands_ref, load_sems, tap_row,
    tx, rx, tx2, rx2, gtx, grx, atx, arx, gall, send_sems, recv_sems,
):
    wide, x_me = lax.axis_index("wide"), lax.axis_index("narrow")
    y_me, z_me, c_me = wide // 8, lax.rem(wide // 2, 4), lax.rem(wide, 2)
    yz_me, cx_me = wide // 2, c_me * 4 + x_me

    def yz_peers():
        for dy, dz in YZ:
            yz = lax.rem(y_me + dy, 4) * 4 + lax.rem(z_me + dz, 4)
            yield yz, (yz * 2 + c_me, x_me)

    def cx_peers():
        for dc, dx in CX:
            c, x = lax.rem(c_me + dc, 2), lax.rem(x_me + dx, 4)
            yield c * 4 + x, (yz_me * 2 + c, x)

    loads = [
        pltpu.make_async_copy(src, dst, load_sems.at[i])
        for i, (src, dst) in enumerate(
            [(frames_hbm, frames_ref), (bands_hbm, bands_ref), (taps_hbm, taps_ref)]
        )
    ]
    for load in loads:
        load.start()

    barrier = pltpu.get_barrier_semaphore()
    for peers in (yz_peers, cx_peers):
        for _, device in peers():
            pl.semaphore_signal(barrier, inc=1, device_id=device, device_id_type=MESH)

    def push(peers, src, dst, slot):
        for p, device in peers():
            pltpu.make_async_remote_copy(
                src_ref=src(p),
                dst_ref=dst,
                send_sem=send_sems.at[slot],
                recv_sem=recv_sems.at[slot],
                device_id=device,
                device_id_type=MESH,
            ).start()

    def wait(ref, count, sem):
        part = ref.at[pl.ds(0, count)]
        pltpu.make_async_copy(part, part, sem).wait()

    for load in loads:
        load.wait()
    colh, coll = bands_ref[0:256, 0:256], bands_ref[0:256, 256:512]
    rowh, rowl = bands_ref[256:384, :], bands_ref[384:512, :]
    x = frames_ref[...].reshape(2 * 2 * 256, 256)
    y = dot(x, colh) + dot(x, coll)
    for p in range(2):
        a = y[p * 256 : (p + 1) * 256]
        b = y[(p + 2) * 256 : (p + 3) * 256]
        right = jnp.concatenate(
            [
                jnp.concatenate([a[:, :128], b[:, :128]], axis=1),
                jnp.concatenate([a[:, 128:], b[:, 128:]], axis=1),
            ],
            axis=0,
        )
        rh, rl = split2(right)
        out = dot(rowh, rh) + (dot(rowh, rl) + dot(rowl, rh))
        tx[8 * p : 8 * p + 8] = out.astype(BF16).reshape(8, 16, 256)

    pl.semaphore_wait(barrier, len(YZ) + len(CX))
    push(yz_peers, lambda p: tx.at[p], rx.at[yz_me], 0)
    rx[yz_me] = tx[yz_me]

    r = lax.broadcasted_iota(jnp.int32, (256, 256), 0)
    c = lax.broadcasted_iota(jnp.int32, (256, 256), 1)
    reorder = jnp.where(c == (r % 16) * 16 + r // 16, 1.0, 0.0).astype(BF16)

    tap_row[...] = jnp.zeros_like(tap_row)
    tap_row[0:1, 0:64] = taps_ref[...].astype(F32)
    base = jnp.broadcast_to(tap_row[0:1, :], (16, 256))
    s_index = lax.broadcasted_iota(jnp.int32, (16, 256), 0)
    t_index = lax.broadcasted_iota(jnp.int32, (16, 256), 1)
    pieces = []
    for v in range(2):
        for cx in range(8):
            rolled = pltpu.roll(base, 2 * cx + v, 1, stride=16, stride_axis=0)
            pieces.append(jnp.where(t_index >= 16 * s_index + 2 * cx + v, rolled, 0.0))
    toeplitz = jnp.concatenate(pieces, axis=0).astype(BF16)

    wait(rx, len(YZ), recv_sems.at[0])
    tx2[...] = dot(reorder, rx[...].reshape(256, 256)).astype(BF16).reshape(8, 32, 256)
    push(cx_peers, lambda p: tx2.at[p], rx2.at[cx_me], 1)
    rx2[cx_me] = tx2[cx_me]
    wait(rx2, len(CX), recv_sems.at[1])
    halves = [rx2[:, 16 * h : 16 * h + 16, :].reshape(128, 256) for h in range(2)]
    received = jnp.concatenate(
        [
            jnp.concatenate([half[:, 128 * v : 128 * v + 128] for half in halves], axis=1)
            for v in range(2)
        ],
        axis=0,
    )
    series = dot(toeplitz, received, 0, 0).astype(BF16)
    series_ref[...] = series

    part = dot(series, series, 1, 1)
    gtx[:, :, 0:128] = part[0:128, 0:128].reshape(16, 8, 128)
    gtx[:, :, 128:256] = part[128:256, 0:128].reshape(16, 8, 128)
    gtx[:, :, 256:384] = part[128:256, 128:256].reshape(16, 8, 128)
    push(yz_peers, lambda p: gtx.at[p], grx.at[yz_me], 2)
    grx[yz_me] = gtx[yz_me]
    wait(grx, len(YZ), recv_sems.at[2])
    atx[...] = jnp.sum(grx[...], axis=0)
    push(cx_peers, lambda p: atx, arx.at[cx_me], 3)
    arx[cx_me] = atx[...]
    wait(arx, len(CX), recv_sems.at[3])
    gall[yz_me] = jnp.sum(arx[...], axis=0)
    push(yz_peers, lambda p: gall.at[yz_me], gall.at[yz_me], 4)
    wait(gall, len(YZ), recv_sems.at[4])
    gram_ref[...] = gall[...].reshape(128, 384) * (1.0 / 32768.0)

    wait(tx, len(YZ), send_sems.at[0])
    wait(tx2, len(CX), send_sems.at[1])
    wait(gtx, len(YZ), send_sems.at[2])
    wait(arx, len(CX), send_sems.at[3])
    wait(gall, len(YZ), send_sems.at[4])


def spread(x):
    return jnp.broadcast_to(x, (8, 128))


def eliminate(matrices):
    tiles = 16
    lane = lax.broadcasted_iota(jnp.int32, (8, 128), 1)
    sub = lax.broadcasted_iota(jnp.int32, (8, 128), 0)
    works = [[g[8 * i : 8 * i + 8] for i in range(tiles)] for g in matrices]
    cols = [[spread(work[0][:, c : c + 1]) for c in range(8)] for work in works]
    for t in range(tiles):
        inside = (lane >= 8 * t) & (lane < 8 * t + 8)
        eye = jnp.where(lane - 8 * t == sub, 1.0, 0.0).astype(F32)
        for m, work in enumerate(works):
            col = cols[m]
            if t + 1 < tiles:
                below = work[t + 1]
                side = [spread(below[:, 8 * t + c : 8 * t + c + 1]) for c in range(8)]
                ahead = [spread(below[:, 8 * t + 8 + c : 8 * t + 9 + c]) for c in range(8)]
                below = jnp.where(inside, 0.0, below)
            base = jnp.where(inside, eye, work[t])
            row = [spread(base[r : r + 1, :]) for r in range(8)]
            inv = [None] * 8
            for s in range(8):
                inv[s] = 1.0 / spread(col[s][s : s + 1, :])
                scaled = row[s] * inv[s]
                if t + 1 < tiles:
                    below = below - side[s] * scaled
                    side_scaled = side[s] * inv[s]
                    for c in range(8):
                        ahead[c] = ahead[c] - side_scaled * spread(side[s][c : c + 1, :])
                for c in range(s + 1, 8):
                    entry = spread(col[s][c : c + 1, :])
                    col[c] = col[c] - (col[s] * entry) * inv[s]
                    row[c] = row[c] - entry * scaled
                    if t + 1 < tiles:
                        side[c] = side[c] - side[s] * (entry * inv[s])
            tile, scale = row[0], inv[0]
            for r in range(1, 8):
                tile = jnp.where(sub == r, row[r], tile)
                scale = jnp.where(sub == r, inv[r], scale)
            if t + 1 < tiles:
                work[t + 1] = below
                cols[m] = ahead
            if t + 2 < tiles:
                ah, am, al = split3(tile)
                bh, bm, bl = split3(tile * scale)
                left = jnp.concatenate([x.astype(F32) for x in (ah, ah, am, ah, al, am)], axis=0)
                right = jnp.concatenate([x.astype(F32) for x in (bh, bm, bh, bl, bh, bm)], axis=0)
                update = dot(left.astype(BF16), right.astype(BF16), 0, 0)
                for i in range(t + 2, tiles):
                    work[i] = jnp.where(inside, 0.0, work[i]) - update[8 * i : 8 * i + 8]
            work[t] = jnp.where(lane < 8 * t + 8, tile * jnp.sqrt(scale), 0.0)
    return [jnp.concatenate(work, axis=0) for work in works]


def factor_kernel(gram_ref, series_ref, sketch_ref, basis_ref, factor_ref):
    c11 = gram_ref[:, 0:128]
    c21 = gram_ref[:, 128:256]
    c22 = gram_ref[:, 256:384]
    cov = jnp.concatenate(
        [jnp.concatenate([c11, c21.T], axis=1), jnp.concatenate([c21, c22], axis=1)], axis=0
    )
    sketch = sketch_ref[...]
    w = dot_fb(cov, sketch)
    g1 = dot_fb(w, sketch, 0, 0).T
    cw = dot_ff(cov, w)
    g2 = dot_ff(w, cw, 0, 0)
    inv1, inv2 = eliminate([g1, g2])
    r = lax.broadcasted_iota(jnp.int32, (128, 128), 0)
    c = lax.broadcasted_iota(jnp.int32, (128, 128), 1)
    upper = jnp.where(c >= r, dot_ff(inv2, g2), 0.0)
    factor_ref[...] = jnp.where(c >= r, dot_ff(upper, inv1, 1, 1), 0.0)
    z = dot_ff(inv2, w, 1, 1)
    basis_ref[...] = dot_fb(z, series_ref[...])


def shards(frames, sketch, kernel_taps):
    narrow_band, broad_band = gauss_band(1.5, 256), gauss_band(3.0, 256)
    colh, coll = np_split2(np.concatenate([narrow_band, broad_band], axis=0).T)
    rowh, rowl = np_split2(np.concatenate([narrow_band, -broad_band], axis=1))
    bands = np.concatenate(
        [np.concatenate([colh, coll], axis=1), np.concatenate([rowh, rowl], axis=0)], axis=0
    )
    vmem = pl.BlockSpec(memory_space=pltpu.VMEM)
    hbm = pl.BlockSpec(memory_space=pltpu.HBM)
    gram, series = pl.pallas_call(
        exchange_kernel,
        out_shape=(
            jax.ShapeDtypeStruct((128, 384), F32),
            jax.ShapeDtypeStruct((256, 256), BF16),
        ),
        in_specs=[hbm] * 3,
        out_specs=(vmem, vmem),
        scratch_shapes=[
            pltpu.VMEM(frames.shape, BF16),
            pltpu.VMEM((1, 64), BF16),
            pltpu.VMEM(bands.shape, BF16),
            pltpu.SemaphoreType.DMA((3,)),
            pltpu.VMEM((8, 256), F32),
            pltpu.VMEM((16, 16, 256), BF16),
            pltpu.VMEM((16, 16, 256), BF16),
            pltpu.VMEM((8, 32, 256), BF16),
            pltpu.VMEM((8, 32, 256), BF16),
            pltpu.VMEM((16, 8, 384), F32),
            pltpu.VMEM((16, 8, 384), F32),
            pltpu.VMEM((8, 384), F32),
            pltpu.VMEM((8, 8, 384), F32),
            pltpu.VMEM((16, 8, 384), F32),
            pltpu.SemaphoreType.DMA((5,)),
            pltpu.SemaphoreType.DMA((5,)),
        ],
        compiler_params=pltpu.CompilerParams(
            collective_id=0, has_side_effects=True, vmem_limit_bytes=56098816
        ),
        name="exchange",
    )(frames, kernel_taps.reshape(1, 64), jnp.asarray(bands))
    return pl.pallas_call(
        factor_kernel,
        out_shape=(jax.ShapeDtypeStruct((128, 256), F32), jax.ShapeDtypeStruct((128, 128), F32)),
        in_specs=[vmem] * 3,
        out_specs=(vmem, vmem),
        compiler_params=pltpu.CompilerParams(vmem_limit_bytes=40 * 2**20),
        name="factorize",
    )(gram, series, sketch)


def solution(mesh):
    return jax.shard_map(
        shards,
        mesh=mesh,
        in_specs=(P(("wide", "narrow"), None, None, None), P(), P()),
        out_specs=(P(None, ("wide", "narrow")), P()),
        check_vma=False,
    )
```

```python
import jax
import jax.numpy as jnp
import numpy as np
from jax import lax
from jax.experimental import pallas as pl
from jax.experimental.pallas import tpu as pltpu
from jax.sharding import PartitionSpec as P

MESH = pl.DeviceIdType.MESH
F32 = jnp.float32
BF16 = jnp.bfloat16


def gauss_band(spread, length):
    position = np.arange(15, dtype=np.float64) - 7.0
    weights = np.exp(-position * position / (2.0 * spread * spread))
    weights = weights / weights.sum()
    matrix = np.zeros((length // 2, length), np.float64)
    for o in range(length // 2):
        for k in range(15):
            c = 2 * o + k - 7
            if 0 <= c < length:
                matrix[o, c] = weights[k]
    return matrix


def split2(matrix):
    hi = matrix.astype(BF16)
    lo = (matrix - hi.astype(F32)).astype(BF16)
    return hi, lo


def split3(matrix):
    hi = matrix.astype(BF16)
    rest = matrix - hi.astype(F32)
    mid = rest.astype(BF16)
    lo = (rest - mid.astype(F32)).astype(BF16)
    return hi, mid, lo


def np_split2(matrix):
    hi = matrix.astype(BF16)
    lo = (matrix - hi.astype(np.float64)).astype(BF16)
    return hi, lo


def dot(a, b, ca=1, cb=0):
    return lax.dot_general(a, b, (((ca,), (cb,)), ((), ())), preferred_element_type=F32)


def dot_ff(a, b, ca=1, cb=0):
    ah, am, al = split3(a)
    bh, bm, bl = split3(b)
    first = dot(ah, bm, ca, cb) + dot(am, bh, ca, cb)
    second = dot(ah, bl, ca, cb) + dot(am, bm, ca, cb) + dot(al, bh, ca, cb)
    return dot(ah, bh, ca, cb) + (first + second)


def dot_fb(a, b, ca=1, cb=0):
    hi, mid, lo = split3(a)
    return dot(hi, b, ca, cb) + (dot(mid, b, ca, cb) + dot(lo, b, ca, cb))


def hops(*offsets):
    return sum(min(o % 4, -o % 4) for o in offsets)


YZ = sorted(((y, z) for y in range(4) for z in range(4) if y or z), key=lambda s: -hops(*s))
CX = sorted(((c, x) for c in range(2) for x in range(4) if c or x), key=lambda s: (-hops(s[1]), -s[0]))


def exchange_kernel(
    frames_hbm, taps_hbm, bands_hbm,
    gram_ref, series_ref,
    frames_ref, taps_ref, bands_ref, load_sems, tap_row,
    tx, rx, tx2, rx2, gtx, grx, atx, arx, gall, send_sems, recv_sems,
):
    wide, x_me = lax.axis_index("wide"), lax.axis_index("narrow")
    y_me, z_me, c_me = wide // 8, lax.rem(wide // 2, 4), lax.rem(wide, 2)
    yz_me, cx_me = wide // 2, c_me * 4 + x_me

    def yz_peers():
        for dy, dz in YZ:
            yz = lax.rem(y_me + dy, 4) * 4 + lax.rem(z_me + dz, 4)
            yield yz, (yz * 2 + c_me, x_me)

    def cx_peers():
        for dc, dx in CX:
            c, x = lax.rem(c_me + dc, 2), lax.rem(x_me + dx, 4)
            yield c * 4 + x, (yz_me * 2 + c, x)

    loads = [
        pltpu.make_async_copy(src, dst, load_sems.at[i])
        for i, (src, dst) in enumerate(
            [(frames_hbm, frames_ref), (bands_hbm, bands_ref), (taps_hbm, taps_ref)]
        )
    ]
    for load in loads:
        load.start()

    barrier = pltpu.get_barrier_semaphore()
    for peers in (yz_peers, cx_peers):
        for _, device in peers():
            pl.semaphore_signal(barrier, inc=1, device_id=device, device_id_type=MESH)

    def push(peers, src, dst, slot):
        for p, device in peers():
            pltpu.make_async_remote_copy(
                src_ref=src(p),
                dst_ref=dst,
                send_sem=send_sems.at[slot],
                recv_sem=recv_sems.at[slot],
                device_id=device,
                device_id_type=MESH,
            ).start()

    def wait(ref, count, sem):
        part = ref.at[pl.ds(0, count)]
        pltpu.make_async_copy(part, part, sem).wait()

    for load in loads:
        load.wait()
    colh, coll = bands_ref[0:256, 0:256], bands_ref[0:256, 256:512]
    rowh, rowl = bands_ref[256:384, :], bands_ref[384:512, :]
    x = frames_ref[...].reshape(2 * 2 * 256, 256)
    y = dot(x, colh) + dot(x, coll)
    for p in range(2):
        a = y[p * 256 : (p + 1) * 256]
        b = y[(p + 2) * 256 : (p + 3) * 256]
        right = jnp.concatenate(
            [
                jnp.concatenate([a[:, :128], b[:, :128]], axis=1),
                jnp.concatenate([a[:, 128:], b[:, 128:]], axis=1),
            ],
            axis=0,
        )
        rh, rl = split2(right)
        out = dot(rowh, rh) + (dot(rowh, rl) + dot(rowl, rh))
        tx[8 * p : 8 * p + 8] = out.astype(BF16).reshape(8, 16, 256)

    pl.semaphore_wait(barrier, len(YZ) + len(CX))
    push(yz_peers, lambda p: tx.at[p], rx.at[yz_me], 0)
    rx[yz_me] = tx[yz_me]

    r = lax.broadcasted_iota(jnp.int32, (256, 256), 0)
    c = lax.broadcasted_iota(jnp.int32, (256, 256), 1)
    reorder = jnp.where(c == (r % 16) * 16 + r // 16, 1.0, 0.0).astype(BF16)

    tap_row[...] = jnp.zeros_like(tap_row)
    tap_row[0:1, 0:64] = taps_ref[...].astype(F32)
    base = jnp.broadcast_to(tap_row[0:1, :], (16, 256))
    s_index = lax.broadcasted_iota(jnp.int32, (16, 256), 0)
    t_index = lax.broadcasted_iota(jnp.int32, (16, 256), 1)
    pieces = []
    for v in range(2):
        for cx in range(8):
            rolled = pltpu.roll(base, 2 * cx + v, 1, stride=16, stride_axis=0)
            pieces.append(jnp.where(t_index >= 16 * s_index + 2 * cx + v, rolled, 0.0))
    toeplitz = jnp.concatenate(pieces, axis=0).astype(BF16)

    wait(rx, len(YZ), recv_sems.at[0])
    tx2[...] = dot(reorder, rx[...].reshape(256, 256)).astype(BF16).reshape(8, 32, 256)
    push(cx_peers, lambda p: tx2.at[p], rx2.at[cx_me], 1)
    rx2[cx_me] = tx2[cx_me]
    wait(rx2, len(CX), recv_sems.at[1])
    halves = [rx2[:, 16 * h : 16 * h + 16, :].reshape(128, 256) for h in range(2)]
    received = jnp.concatenate(
        [
            jnp.concatenate([half[:, 128 * v : 128 * v + 128] for half in halves], axis=1)
            for v in range(2)
        ],
        axis=0,
    )
    series = dot(toeplitz, received, 0, 0).astype(BF16)
    series_ref[...] = series

    part = dot(series, series, 1, 1)
    first, second = part[0:128, 0:128], part[128:256, 128:256]
    r = lax.broadcasted_iota(jnp.int32, (128, 128), 0)
    c = lax.broadcasted_iota(jnp.int32, (128, 128), 1)
    diagonal = jnp.sum(jnp.where(r == c, second, 0.0), axis=0, keepdims=True)
    gtx[:, 0:8, :] = jnp.where(r >= c, first, second).reshape(16, 8, 128)
    gtx[:, 8:16, :] = part[128:256, 0:128].reshape(16, 8, 128)
    gtx[:, 16:17, :] = jnp.broadcast_to(diagonal.reshape(1, 1, 128), (16, 1, 128))
    push(yz_peers, lambda p: gtx.at[p], grx.at[yz_me], 2)
    grx[yz_me] = gtx[yz_me]
    wait(grx, len(YZ), recv_sems.at[2])
    atx[...] = jnp.sum(grx[...], axis=0)
    push(cx_peers, lambda p: atx, arx.at[cx_me], 3)
    arx[cx_me] = atx[...]
    wait(arx, len(CX), recv_sems.at[3])
    gall[yz_me] = jnp.sum(arx[...], axis=0) * (1.0 / 32768.0)
    push(yz_peers, lambda p: gall.at[yz_me], gall.at[yz_me], 4)
    wait(gall, len(YZ), recv_sems.at[4])
    gram_ref[0:128, 0:128] = gall[:, 0:8, :].reshape(128, 128)
    gram_ref[0:128, 128:256] = gall[:, 8:16, :].reshape(128, 128)
    gram_ref[128:136, 0:128] = jnp.broadcast_to(gall[0, 16:17, :], (8, 128))
    gram_ref[128:136, 128:256] = jnp.zeros((8, 128), F32)

    wait(tx, len(YZ), send_sems.at[0])
    wait(tx2, len(CX), send_sems.at[1])
    wait(gtx, len(YZ), send_sems.at[2])
    wait(arx, len(CX), send_sems.at[3])
    wait(gall, len(YZ), send_sems.at[4])


def spread(x):
    return jnp.broadcast_to(x, (8, 128))


def eliminate(matrices):
    tiles = 16
    lane = lax.broadcasted_iota(jnp.int32, (8, 128), 1)
    sub = lax.broadcasted_iota(jnp.int32, (8, 128), 0)
    works = [[g[8 * i : 8 * i + 8] for i in range(tiles)] for g in matrices]
    cols = [[spread(work[0][:, c : c + 1]) for c in range(8)] for work in works]
    for t in range(tiles):
        inside = (lane >= 8 * t) & (lane < 8 * t + 8)
        eye = jnp.where(lane - 8 * t == sub, 1.0, 0.0).astype(F32)
        for m, work in enumerate(works):
            col = cols[m]
            if t + 1 < tiles:
                below = work[t + 1]
                side = [spread(below[:, 8 * t + c : 8 * t + c + 1]) for c in range(8)]
                ahead = [spread(below[:, 8 * t + 8 + c : 8 * t + 9 + c]) for c in range(8)]
                below = jnp.where(inside, 0.0, below)
            base = jnp.where(inside, eye, work[t])
            row = [spread(base[r : r + 1, :]) for r in range(8)]
            inv = [None] * 8
            for s in range(8):
                inv[s] = 1.0 / spread(col[s][s : s + 1, :])
                scaled = row[s] * inv[s]
                if t + 1 < tiles:
                    below = below - side[s] * scaled
                    side_scaled = side[s] * inv[s]
                    for c in range(8):
                        ahead[c] = ahead[c] - side_scaled * spread(side[s][c : c + 1, :])
                for c in range(s + 1, 8):
                    entry = spread(col[s][c : c + 1, :])
                    col[c] = col[c] - (col[s] * entry) * inv[s]
                    row[c] = row[c] - entry * scaled
                    if t + 1 < tiles:
                        side[c] = side[c] - side[s] * (entry * inv[s])
            tile, scale = row[0], inv[0]
            for r in range(1, 8):
                tile = jnp.where(sub == r, row[r], tile)
                scale = jnp.where(sub == r, inv[r], scale)
            if t + 1 < tiles:
                work[t + 1] = below
                cols[m] = ahead
            if t + 2 < tiles:
                ah, am, al = split3(tile)
                bh, bm, bl = split3(tile * scale)
                left = jnp.concatenate([x.astype(F32) for x in (ah, ah, am, ah, al, am)], axis=0)
                right = jnp.concatenate([x.astype(F32) for x in (bh, bm, bh, bl, bh, bm)], axis=0)
                update = dot(left.astype(BF16), right.astype(BF16), 0, 0)
                for i in range(t + 2, tiles):
                    work[i] = jnp.where(inside, 0.0, work[i]) - update[8 * i : 8 * i + 8]
            work[t] = jnp.where(lane < 8 * t + 8, tile * jnp.sqrt(scale), 0.0)
    return [jnp.concatenate(work, axis=0) for work in works]


def factor_kernel(gram_ref, series_ref, sketch_ref, basis_ref, factor_ref):
    r = lax.broadcasted_iota(jnp.int32, (128, 128), 0)
    c = lax.broadcasted_iota(jnp.int32, (128, 128), 1)
    both, c21, diagonal = gram_ref[0:128, 0:128], gram_ref[0:128, 128:256], gram_ref[128:129, 0:128]
    turned = both.T
    c11 = jnp.where(r >= c, both, turned)
    c22 = jnp.where(r < c, both, jnp.where(r == c, diagonal, turned))
    cov = jnp.concatenate(
        [jnp.concatenate([c11, c21.T], axis=1), jnp.concatenate([c21, c22], axis=1)], axis=0
    )
    sketch = sketch_ref[...]
    w = dot_fb(cov, sketch)
    g1 = dot_fb(w, sketch, 0, 0).T
    cw = dot_ff(cov, w)
    g2 = dot_ff(w, cw, 0, 0)
    inv1, inv2 = eliminate([g1, g2])
    upper = jnp.where(c >= r, dot_ff(inv2, g2), 0.0)
    factor_ref[...] = jnp.where(c >= r, dot_ff(upper, inv1, 1, 1), 0.0)
    z = dot_ff(inv2, w, 1, 1)
    basis_ref[...] = dot_fb(z, series_ref[...])


def shards(frames, sketch, kernel_taps):
    narrow_band, broad_band = gauss_band(1.5, 256), gauss_band(3.0, 256)
    colh, coll = np_split2(np.concatenate([narrow_band, broad_band], axis=0).T)
    rowh, rowl = np_split2(np.concatenate([narrow_band, -broad_band], axis=1))
    bands = np.concatenate(
        [np.concatenate([colh, coll], axis=1), np.concatenate([rowh, rowl], axis=0)], axis=0
    )
    vmem = pl.BlockSpec(memory_space=pltpu.VMEM)
    hbm = pl.BlockSpec(memory_space=pltpu.HBM)
    gram, series = pl.pallas_call(
        exchange_kernel,
        out_shape=(
            jax.ShapeDtypeStruct((136, 256), F32),
            jax.ShapeDtypeStruct((256, 256), BF16),
        ),
        in_specs=[hbm] * 3,
        out_specs=(vmem, vmem),
        scratch_shapes=[
            pltpu.VMEM(frames.shape, BF16),
            pltpu.VMEM((1, 64), BF16),
            pltpu.VMEM(bands.shape, BF16),
            pltpu.SemaphoreType.DMA((3,)),
            pltpu.VMEM((8, 256), F32),
            pltpu.VMEM((16, 16, 256), BF16),
            pltpu.VMEM((16, 16, 256), BF16),
            pltpu.VMEM((8, 32, 256), BF16),
            pltpu.VMEM((8, 32, 256), BF16),
            pltpu.VMEM((16, 17, 128), F32),
            pltpu.VMEM((16, 17, 128), F32),
            pltpu.VMEM((17, 128), F32),
            pltpu.VMEM((8, 17, 128), F32),
            pltpu.VMEM((16, 17, 128), F32),
            pltpu.SemaphoreType.DMA((5,)),
            pltpu.SemaphoreType.DMA((5,)),
        ],
        compiler_params=pltpu.CompilerParams(
            collective_id=0, has_side_effects=True, vmem_limit_bytes=56098816
        ),
        name="exchange",
    )(frames, pltpu.with_memory_space_constraint(kernel_taps.reshape(1, 64), pltpu.HBM), jnp.asarray(bands))
    return pl.pallas_call(
        factor_kernel,
        out_shape=(jax.ShapeDtypeStruct((128, 256), F32), jax.ShapeDtypeStruct((128, 128), F32)),
        in_specs=[vmem] * 3,
        out_specs=(vmem, vmem),
        compiler_params=pltpu.CompilerParams(vmem_limit_bytes=40 * 2**20),
        name="factorize",
    )(gram, series, sketch)


def solution(mesh):
    return jax.shard_map(
        shards,
        mesh=mesh,
        in_specs=(P(("wide", "narrow"), None, None, None), P(), P()),
        out_specs=(P(None, ("wide", "narrow")), P()),
        check_vma=False,
    )
```
